32 devices in a mesh: ctx: 8 (over y, x, core), tp: 4 (over z).
Axes of the slice: x: 2, y: 2, z: 4, core: 2. Of those that a mesh axis runs over, the one named last changes fastest.
Arguments:
- tokens: bfloat16 [8, 1024, 768], P(None, 'ctx'), may hold values from -6 to 6
- cotangent: bfloat16 [8, 1024, 768], P(None, 'ctx'), may hold values from -1.5 to 1.5
- seq_lengths: int32 [8], replicated, may hold values from 256 to 1024, as said below
- combined_weight: bfloat16 [2, 768, 12, 3, 64], P(None, None, 'tp'), may hold values from -0.21875 to 0.21875
- joined_bias: bfloat16 [2, 12, 2, 64], P(None, 'tp'), may hold values from -3 to 3
- attention_out_weight: bfloat16 [2, 768, 768], P(None, 'tp'), may hold values from -9 to 9
- attention_out_bias: bfloat16 [2, 768], replicated, may hold values from -3 to 3
- expand_weight: bfloat16 [2, 768, 3072], P(None, None, 'tp'), may hold values from -0.21875 to 0.21875
- expand_bias: bfloat16 [2, 3072], P(None, 'tp'), may hold values from -3 to 3
- contract_weight: bfloat16 [2, 3072, 768], P(None, 'tp'), may hold values from -0.109375 to 0.109375
- contract_bias: bfloat16 [2, 768], replicated, may hold values from -3 to 3
- norm_gains: bfloat16 [2, 2, 768], replicated, may hold values from 0.25 to 1.75
- norm_shifts: bfloat16 [2, 2, 768], replicated, may hold values from -3 to 3
Outputs:
- outputs: float32 [8, 1024, 768], P(None, 'ctx')
- tokens_grad: float32 [8, 1024, 768], P(None, 'ctx')
- grad_joined: float32 [2, 768, 12, 3, 64], P(None, None, 'tp')
- grad_qvbias: float32 [2, 12, 2, 64], P(None, 'tp')
- grad_mixer: float32 [2, 768, 768], P(None, 'tp')
- grad_mbias: float32 [2, 768], replicated
- grad_upward: float32 [2, 768, 3072], P(None, None, 'tp')
- grad_ubias: float32 [2, 3072], P(None, 'tp')
- grad_down: float32 [2, 3072, 768], P(None, 'tp')
- grad_dbias: float32 [2, 768], replicated
- grad_gains: float32 [2, 2, 768], replicated
- grad_shifts: float32 [2, 2, 768], replicated
The draws below stay inside these ranges and needn't reach their ends.
Inputs may be any that keep to these rules, and one draw needn't show every extreme that they name: `seq_lengths`: at least one sequence has length 1024 in every draw.
All inputs are finite; a program needn't handle non-finite values.
Results may differ from the reference program's by a relative error of at most 0.018.
Values may be sent and summed in bfloat16 or wider, within the bound.
A program may use at most 448 MiB of HBM per device.

```python
import jax
import jax.numpy as jnp
from jax import lax

D = 768
HEADS = 12
HD = 64
FF = 3072
LAYERS = 2
SEQS = 8
LENGTH = 1024


def draw_seq_lengths(key, part):
    base = jax.random.randint(jax.random.fold_in(key, 11), (SEQS,), LENGTH // 4, LENGTH + 1)
    chosen = jax.random.randint(jax.random.fold_in(key, 12), (), 0, SEQS)
    return jnp.where(jnp.arange(SEQS) == chosen, LENGTH, base).astype(jnp.int32)


def shard_levels(own_key, extent, shards, least, largest):
    def one(dim, shards_of):
        heights = jax.random.uniform(jax.random.fold_in(jax.random.fold_in(own_key, 6), dim), (shards_of,), jnp.float32, least / len(shards), largest / len(shards))
        return jnp.repeat(jnp.exp(heights), extent[dim] // shards_of).reshape((-1,) + (1,) * (len(extent) - dim - 1))

    level = one(*shards[0])
    for cut in shards[1:]:
        level = level * one(*cut)
    return level


def noise(key, dims, scale, reach, split=(), held_as=jnp.bfloat16):
    gain = shard_levels(key, dims, split, -0.22, 0.18) if split else 1.0
    array = jax.random.normal(key, dims, jnp.float32) * scale * gain
    return jnp.minimum(jnp.maximum(array, -reach), reach).astype(held_as)


def setup_inputs(seed: int = 0) -> dict:
    streams_of = jax.random.split(jax.random.key(seed), 14)
    return {
        "tokens": noise(streams_of[0], (SEQS, LENGTH, D), 1.0, 6.0, ((1, 8),)),
        "cotangent": noise(streams_of[1], (SEQS, LENGTH, D), 0.25, 1.5, ((1, 8),)),
        "seq_lengths": draw_seq_lengths(jax.random.fold_in(streams_of[13], 71), 0),
        "combined_weight": noise(streams_of[3], (LAYERS, D, HEADS, 3, HD), D ** -0.5, 0.21875, ((2, 4),)),
        "joined_bias": noise(streams_of[4], (LAYERS, HEADS, 2, HD), 0.5, 3.0, ((1, 4),)),
        "attention_out_weight": noise(streams_of[5], (LAYERS, D, D), 1.5, 9.0, ((1, 4),)),
        "attention_out_bias": noise(streams_of[6], (LAYERS, D), 0.5, 3.0),
        "expand_weight": noise(streams_of[7], (LAYERS, D, FF), D ** -0.5, 0.21875, ((2, 4),)),
        "expand_bias": noise(streams_of[8], (LAYERS, FF), 0.5, 3.0, ((1, 4),)),
        "contract_weight": noise(streams_of[9], (LAYERS, FF, D), FF ** -0.5, 0.109375, ((1, 4),)),
        "contract_bias": noise(streams_of[10], (LAYERS, D), 0.5, 3.0),
        "norm_gains": jnp.clip(1.0 + 0.15 * jax.random.normal(streams_of[11], (LAYERS, 2, D), jnp.float32), 0.25, 1.75).astype(jnp.bfloat16),
        "norm_shifts": noise(streams_of[12], (LAYERS, 2, D), 0.5, 3.0),
    }


EPS = 1e-12
MASKED = -1e+30
FULL_ACCURACY = lax.Precision.HIGHEST

@jax.custom_vjp
def low(v):
    return lax.optimization_barrier(v.astype(jnp.bfloat16)).astype(jnp.float32)

@jax.custom_vjp
def low_back(v):
    return v

def low_keep(v):
    return (low(v), None)

def low_pass(kept, grad):
    return (grad,)

def back_keep(v):
    return (v, None)

def back_low(kept, grad):
    return (low(grad),)
low.defvjp(low_keep, low_pass)
low_back.defvjp(back_keep, back_low)

def normalize(resid, norm_gain, norm_shift):
    row_mean = lax.optimization_barrier(jnp.mean(resid, axis=-1, keepdims=True))
    centred = resid - row_mean
    spread = lax.optimization_barrier(jnp.mean(centred * centred, axis=-1, keepdims=True))
    return centred * lax.rsqrt(spread + EPS) * norm_gain + norm_shift

def smooth_gate(value):
    return 0.5 * value * (1.0 + jnp.tanh(0.7978845608028654 * (value + 0.044715 * value * value * value)))

def attend_sequence(queries, key_rows, value_rows, seq_len):
    block_rows = min(512, LENGTH)
    key_valid = jnp.arange(LENGTH) < seq_len

    def one_block(query_block):
        scores = jnp.einsum('qhd,khd->hqk', query_block, key_rows, precision=FULL_ACCURACY)
        scores = low_back(scores * HD ** (-0.5))
        scores = jnp.where(key_valid[None, None, :], scores, MASKED)
        row_max = lax.optimization_barrier(jnp.max(scores, axis=-1, keepdims=True))
        exp_terms = jnp.exp(scores - row_max)
        attn_probs = low(exp_terms / lax.optimization_barrier(jnp.sum(exp_terms, axis=-1, keepdims=True)))
        return jnp.einsum('hqk,khd->qhd', attn_probs, value_rows, precision=FULL_ACCURACY)
    blocks = queries.reshape(LENGTH // block_rows, block_rows, HEADS, HD)
    return lax.map(jax.checkpoint(one_block), blocks).reshape(LENGTH, HEADS, HD)

def per_sequence(operands):
    return attend_sequence(operands[0], operands[1], operands[2], operands[3])

def layer(hidden, seq_lengths, combined_weight, joined_bias, attention_out_weight, attention_out_bias, expand_weight, expand_bias, contract_weight, contract_bias, norm_gains, norm_shifts):
    hidden_reduced = low(hidden)
    combined_projected = jnp.einsum('zqo,okgm->zqkgm', hidden_reduced, combined_weight, precision=FULL_ACCURACY)
    queries = low_back(low(combined_projected[..., 0, :] + joined_bias[:, 0, :]))
    key_rows = low_back(low(combined_projected[..., 1, :]))
    value_rows = low_back(low(combined_projected[..., 2, :] + joined_bias[:, 1, :]))
    heads_out = lax.map(jax.checkpoint(per_sequence), (queries, key_rows, value_rows, seq_lengths))
    merged_head_output = low_back(low(heads_out.reshape(SEQS, LENGTH, D)))
    attention_branch = low_back(jnp.einsum('iwf,fp->iwp', merged_head_output, attention_out_weight, precision=FULL_ACCURACY)) + attention_out_bias
    normalized_rows = normalize(hidden + attention_branch, norm_gains[0], norm_shifts[0])
    before_activation = low_back(jnp.einsum('eik,ku->eiu', low(normalized_rows), expand_weight, precision=FULL_ACCURACY) + expand_bias)
    activated_hidden = low(smooth_gate(before_activation))
    feedforward_branch = low_back(jnp.einsum('nbg,gh->nbh', activated_hidden, contract_weight, precision=FULL_ACCURACY)) + contract_bias
    return normalize(normalized_rows + feedforward_branch, norm_gains[1], norm_shifts[1])

def reference(tokens, cotangent, seq_lengths, combined_weight, joined_bias, attention_out_weight, attention_out_bias, expand_weight, expand_bias, contract_weight, contract_bias, norm_gains, norm_shifts):
    weights = tuple((weight.astype(jnp.float32) for weight in (combined_weight, joined_bias, attention_out_weight, attention_out_bias, expand_weight, expand_bias, contract_weight, contract_bias, norm_gains, norm_shifts)))

    def forward(hidden, *params):
        for layer_idx in range(LAYERS):
            hidden = layer(hidden, seq_lengths, *[weight[layer_idx] for weight in params])
        return hidden
    outputs, pullback = jax.vjp(forward, tokens.astype(jnp.float32), *weights)
    grads = pullback(cotangent.astype(jnp.float32))
    return (outputs, grads[0], grads[1], grads[2], grads[3], grads[4], grads[5], grads[6], grads[7], grads[8], grads[9], grads[10])
```

```python
import jax
import jax.numpy as jnp
from jax import lax
from jax.sharding import PartitionSpec as P

EPS = 1e-12
MASKED = -1e30


def normalize(resid, norm_gain, norm_shift):
    row_mean = jnp.mean(resid, axis=-1, keepdims=True)
    centred = resid - row_mean
    spread = jnp.mean(centred * centred, axis=-1, keepdims=True)
    return centred * lax.rsqrt(spread + EPS) * norm_gain + norm_shift


def smooth_gate(value):
    return (
        0.5
        * value
        * (1.0 + jnp.tanh(0.7978845608028654 * (value + 0.044715 * value * value * value)))
    )


def attention_scores(queries, key_rows, key_valid, scale):
    scores = (
        jnp.einsum("sqhd,skhd->shqk", queries, key_rows, preferred_element_type=jnp.float32) * scale
    )
    return jnp.where(key_valid[:, None, None, :], scores, MASKED)


def share_sum(partial_rows):
    return lax.psum_scatter(partial_rows, "tp", scatter_dimension=1, tiled=True)


def share_gather(rows_low):
    return lax.all_gather(rows_low, "tp", axis=1, tiled=True)


def take_share(full_rows):
    share_rows = full_rows.shape[1] // lax.axis_size("tp")
    return lax.dynamic_slice_in_dim(full_rows, lax.axis_index("tp") * share_rows, share_rows, 1)


def forward_layer(
    hidden,
    hidden_reduced,
    seq_lengths,
    combined_weight,
    joined_bias,
    attention_out_weight,
    attention_out_bias,
    expand_weight,
    expand_bias,
    contract_weight,
    contract_bias,
    norm_gains,
    norm_shifts,
):
    n_seqs, n_rows, width = hidden_reduced.shape
    n_heads = combined_weight.shape[1]
    head_dim = combined_weight.shape[3]
    scale = head_dim ** (-0.5)
    joined_flat = combined_weight.reshape(width, -1)
    combined_projected = jnp.einsum(
        "sbd,dc->sbc", hidden_reduced, joined_flat, preferred_element_type=jnp.float32
    )
    combined_projected = combined_projected.reshape(n_seqs, n_rows, n_heads, 3, head_dim)
    queries = (combined_projected[..., 0, :] + joined_bias[:, 0, :]).astype(jnp.bfloat16)
    key_rows = combined_projected[..., 1, :].astype(jnp.bfloat16)
    value_rows = (combined_projected[..., 2, :] + joined_bias[:, 1, :]).astype(jnp.bfloat16)
    all_keys, all_values = (
        lax.all_gather(key_rows.reshape(n_seqs, n_rows, -1), "ctx", axis=1, tiled=True),
        lax.all_gather(value_rows.reshape(n_seqs, n_rows, -1), "ctx", axis=1, tiled=True),
    )
    total_len = all_keys.shape[1]
    all_keys = all_keys.reshape(n_seqs, total_len, n_heads, head_dim)
    all_values = all_values.reshape(n_seqs, total_len, n_heads, head_dim)
    key_valid = jnp.arange(total_len)[None, :] < seq_lengths[:, None]
    scores = attention_scores(queries, all_keys, key_valid, scale)
    row_max = jnp.max(scores, axis=-1, keepdims=True)
    log_total = row_max + jnp.log(jnp.sum(jnp.exp(scores - row_max), axis=-1, keepdims=True))
    attn_probs = jnp.exp(scores - log_total).astype(jnp.bfloat16)
    merged_head_output = jnp.einsum(
        "shqk,skhd->sqhd", attn_probs, all_values, preferred_element_type=jnp.float32
    )
    merged_head_output = merged_head_output.astype(jnp.bfloat16).reshape(n_seqs, n_rows, -1)
    attention_branch = jnp.einsum(
        "sbc,cd->sbd", merged_head_output, attention_out_weight, preferred_element_type=jnp.float32
    )
    attention_branch = share_sum(attention_branch)
    normalized_rows, first_back = jax.vjp(
        normalize, hidden + attention_branch + attention_out_bias, norm_gains[0], norm_shifts[0]
    )
    normed_low = normalized_rows.astype(jnp.bfloat16)
    normed_low = share_gather(normed_low)
    before_activation = (
        jnp.einsum("sbd,df->sbf", normed_low, expand_weight, preferred_element_type=jnp.float32)
        + expand_bias
    )
    activated_hidden, gate_back = jax.vjp(smooth_gate, before_activation)
    gated_low = activated_hidden.astype(jnp.bfloat16)
    feedforward_branch = jnp.einsum(
        "sbf,fd->sbd", gated_low, contract_weight, preferred_element_type=jnp.float32
    )
    feedforward_branch = share_sum(feedforward_branch)
    result, second_back = jax.vjp(
        normalize,
        normalized_rows + feedforward_branch + contract_bias,
        norm_gains[1],
        norm_shifts[1],
    )
    kept = (
        hidden_reduced,
        queries,
        key_rows,
        value_rows,
        all_keys,
        all_values,
        key_valid,
        log_total,
        merged_head_output,
        normed_low,
        gated_low,
        first_back,
        gate_back,
        second_back,
    )
    return (result, kept)


def backward_layer(
    grad_out, kept, combined_weight, attention_out_weight, expand_weight, contract_weight
):
    (
        hidden_reduced,
        queries,
        key_rows,
        value_rows,
        all_keys,
        all_values,
        key_valid,
        log_total,
        merged_head_output,
        normed_low,
        gated_low,
        first_back,
        gate_back,
        second_back,
    ) = kept
    n_seqs, n_rows, n_heads, head_dim = queries.shape
    width = hidden_reduced.shape[2]
    total_len = all_keys.shape[1]
    scale = head_dim ** (-0.5)
    d_resid_two, d_gain_two, d_shift_two = second_back(grad_out)
    d_down_bias = jnp.sum(d_resid_two, axis=(0, 1))
    d_branch_two = d_resid_two.astype(jnp.bfloat16)
    d_branch_two = share_gather(d_branch_two)
    d_down = jnp.einsum("sbf,sbd->fd", gated_low, d_branch_two, preferred_element_type=jnp.float32)
    d_gated = jnp.einsum(
        "sbd,fd->sbf", d_branch_two, contract_weight, preferred_element_type=jnp.float32
    )
    d_pre_gate = gate_back(d_gated)[0].astype(jnp.bfloat16)
    d_up_bias = jnp.sum(d_pre_gate.astype(jnp.float32), axis=(0, 1))
    d_upward = jnp.einsum("sbd,sbf->df", normed_low, d_pre_gate, preferred_element_type=jnp.float32)
    d_normed = jnp.einsum(
        "sbf,df->sbd", d_pre_gate, expand_weight, preferred_element_type=jnp.float32
    )
    d_normed = share_sum(d_normed) + d_resid_two
    d_resid_one, d_gain_one, d_shift_one = first_back(d_normed)
    d_mixer_bias = jnp.sum(d_resid_one, axis=(0, 1))
    d_branch = d_resid_one.astype(jnp.bfloat16)
    d_branch = share_gather(d_branch)
    d_mixer = jnp.einsum(
        "sbc,sbd->cd", merged_head_output, d_branch, preferred_element_type=jnp.float32
    )
    d_mixed = jnp.einsum(
        "sbd,cd->sbc", d_branch, attention_out_weight, preferred_element_type=jnp.float32
    )
    d_mixed = d_mixed.astype(jnp.bfloat16).reshape(n_seqs, n_rows, n_heads, head_dim)
    scores = attention_scores(queries, all_keys, key_valid, scale)
    probs_full = jnp.exp(scores - log_total)
    d_probs = jnp.einsum("sqhd,skhd->shqk", d_mixed, all_values, preferred_element_type=jnp.float32)
    row_delta = jnp.sum(probs_full * d_probs, axis=-1, keepdims=True)
    d_scores = (probs_full * (d_probs - row_delta)).astype(jnp.bfloat16)
    d_queries = (
        jnp.einsum("shqk,skhd->sqhd", d_scores, all_keys, preferred_element_type=jnp.float32)
        * scale
    )
    d_queries = d_queries.astype(jnp.bfloat16)
    key_part = (
        jnp.einsum("shqk,sqhd->skhd", d_scores, queries, preferred_element_type=jnp.float32) * scale
    )
    value_part = jnp.einsum(
        "shqk,sqhd->skhd",
        probs_full.astype(jnp.bfloat16),
        d_mixed,
        preferred_element_type=jnp.float32,
    )
    d_keys, d_values = (
        lax.psum_scatter(
            key_part.reshape(n_seqs, total_len, -1), "ctx", scatter_dimension=1, tiled=True
        ),
        lax.psum_scatter(
            value_part.reshape(n_seqs, total_len, -1), "ctx", scatter_dimension=1, tiled=True
        ),
    )
    d_keys = d_keys.reshape(n_seqs, n_rows, n_heads, head_dim)
    d_values = d_values.reshape(n_seqs, n_rows, n_heads, head_dim)
    d_keys = d_keys.astype(jnp.bfloat16)
    d_values = d_values.astype(jnp.bfloat16)
    d_joined_bias = jnp.stack(
        [
            jnp.sum(d_queries.astype(jnp.float32), axis=(0, 1)),
            jnp.sum(d_values.astype(jnp.float32), axis=(0, 1)),
        ],
        axis=1,
    )
    d_joined_out = jnp.stack([d_queries, d_keys, d_values], axis=3).reshape(n_seqs, n_rows, -1)
    d_joined = jnp.einsum(
        "sbd,sbc->dc", hidden_reduced, d_joined_out, preferred_element_type=jnp.float32
    )
    d_joined = d_joined.reshape(width, n_heads, 3, head_dim)
    d_hidden = jnp.einsum(
        "sbc,dc->sbd",
        d_joined_out,
        combined_weight.reshape(width, -1),
        preferred_element_type=jnp.float32,
    )
    d_hidden = share_sum(d_hidden) + d_resid_one
    small_grads = (
        d_mixer_bias,
        d_down_bias,
        jnp.stack([d_gain_one, d_gain_two]),
        jnp.stack([d_shift_one, d_shift_two]),
    )
    small_grads = lax.psum(
        (
            small_grads[0],
            small_grads[1],
            small_grads[2].astype(jnp.float32),
            small_grads[3].astype(jnp.float32),
        ),
        "tp",
    )
    grads = (
        d_joined,
        d_joined_bias,
        d_mixer,
        small_grads[0],
        d_upward,
        d_up_bias,
        d_down,
        small_grads[1],
        small_grads[2],
        small_grads[3],
    )
    return (d_hidden, grads)


def sum_layer(grads):
    return lax.psum(
        (
            grads[0],
            grads[1],
            grads[2],
            grads[3],
            grads[4],
            grads[5],
            grads[6],
            grads[7],
            grads[8],
            grads[9],
        ),
        "ctx",
    )


def on_device(
    tokens,
    cotangent,
    seq_lengths,
    combined_weight,
    joined_bias,
    attention_out_weight,
    attention_out_bias,
    expand_weight,
    expand_bias,
    contract_weight,
    contract_bias,
    norm_gains,
    norm_shifts,
):
    params = (
        combined_weight,
        joined_bias,
        attention_out_weight,
        attention_out_bias,
        expand_weight,
        expand_bias,
        contract_weight,
        contract_bias,
        norm_gains,
        norm_shifts,
    )
    n_layers = combined_weight.shape[0]
    hidden = tokens.astype(jnp.float32)
    hidden_reduced = tokens
    hidden = take_share(hidden)
    saved = []
    for layer_idx in range(n_layers):
        hidden, kept = forward_layer(
            hidden, hidden_reduced, seq_lengths, *[weight[layer_idx] for weight in params]
        )
        saved.append(kept)
        if layer_idx + 1 < n_layers:
            hidden_reduced = hidden.astype(jnp.bfloat16)
            hidden_reduced = share_gather(hidden_reduced)
    grad_now = cotangent.astype(jnp.float32)
    grad_now = take_share(grad_now)
    collected = []
    for layer_idx in reversed(range(n_layers)):
        grad_now, grads = backward_layer(
            grad_now,
            saved[layer_idx],
            combined_weight[layer_idx],
            attention_out_weight[layer_idx],
            expand_weight[layer_idx],
            contract_weight[layer_idx],
        )
        grads = sum_layer(grads)
        collected.insert(0, grads)
    stacked = tuple((jnp.stack([entry[member] for entry in collected]) for member in range(10)))
    hidden, grad_now = (
        lax.all_gather(hidden, "tp", axis=1, tiled=True),
        lax.all_gather(grad_now, "tp", axis=1, tiled=True),
    )
    return (
        hidden,
        grad_now,
        stacked[0],
        stacked[1],
        stacked[2],
        stacked[3],
        stacked[4],
        stacked[5],
        stacked[6],
        stacked[7],
        stacked[8],
        stacked[9],
    )

def rows_of(array, axis_name, dim):
    share = array.shape[dim] // lax.axis_size(axis_name)
    return lax.dynamic_slice_in_dim(array, lax.axis_index(axis_name) * share, share, dim)


def after(value, *earlier):
    return lax.optimization_barrier((value,) + earlier)[0]


def fetch_columns(weight):
    part = lax.all_gather(rows_of(weight, "ctx", 0), "tp", axis=0)
    part = part.transpose(1, 0, 2).reshape(part.shape[1], -1)
    return lax.all_gather(part, "ctx", axis=0, tiled=True)


def fetch_rows(weight):
    part = lax.all_gather(rows_of(weight, "ctx", 0), "tp", axis=0)
    whole = lax.all_gather(part, "ctx", axis=1, tiled=True)
    return whole.reshape(-1, whole.shape[2])


def reduce_columns(grad):
    n_tp = lax.axis_size("tp")
    part = lax.psum_scatter(grad.astype(jnp.bfloat16), "ctx", scatter_dimension=0, tiled=True)
    part = part.reshape(part.shape[0], n_tp, -1).transpose(1, 0, 2)
    return lax.psum_scatter(part, "tp", scatter_dimension=0)


def reduce_rows(grad):
    n_tp = lax.axis_size("tp")
    part = grad.astype(jnp.bfloat16).reshape(n_tp, -1, grad.shape[1])
    part = lax.psum_scatter(part, "ctx", scatter_dimension=1, tiled=True)
    return lax.psum_scatter(part, "tp", scatter_dimension=0)


def spread(part):
    return lax.all_gather(part, "ctx", axis=0, tiled=True).astype(jnp.float32)


def to_heads(rows, n_groups):
    n_rows = rows.shape[0] * n_groups // lax.axis_size("ctx")
    blocks = rows.reshape(-1, n_rows, n_groups, rows.shape[1] // n_groups)
    blocks = blocks.transpose(0, 2, 1, 3).reshape(-1, n_rows, blocks.shape[3])
    blocks = lax.all_to_all(blocks, "ctx", 0, 0, tiled=True)
    return blocks.reshape(-1, blocks.shape[2])


def to_rows(whole, n_groups):
    n_ctx = lax.axis_size("ctx")
    blocks = whole.reshape(n_ctx, whole.shape[0] // n_ctx, whole.shape[1])
    blocks = lax.all_to_all(blocks, "ctx", 0, 0, tiled=True)
    blocks = blocks.reshape(n_ctx // n_groups, n_groups, blocks.shape[1], blocks.shape[2])
    blocks = blocks.transpose(0, 2, 1, 3)
    return blocks.reshape(-1, n_groups * whole.shape[1])


def matmul(left, right):
    return jnp.dot(left, right, preferred_element_type=jnp.float32)


def matmul_tn(left, right):
    return lax.dot_general(left, right, (((0,), (0,)), ((), ())), preferred_element_type=jnp.float32)


def matmul_nt(left, right):
    return lax.dot_general(left, right, (((1,), (1,)), ((), ())), preferred_element_type=jnp.float32)


def attend(joined, key_valid, head_dim):
    total_len = joined.shape[0]
    scale = head_dim ** (-0.5)
    parts = joined.reshape(total_len, -1, 3, head_dim).transpose(2, 1, 0, 3)
    queries, keys, values = parts[0], parts[1], parts[2]
    scores = jnp.einsum("hqd,hkd->hqk", queries, keys, preferred_element_type=jnp.float32) * scale
    scores = jnp.where(key_valid[None, None, :], scores, MASKED)
    row_max = jnp.max(scores, axis=-1, keepdims=True)
    log_total = row_max + jnp.log(jnp.sum(jnp.exp(scores - row_max), axis=-1, keepdims=True))
    probs = jnp.exp(scores - log_total).astype(jnp.bfloat16)
    mixed = jnp.einsum("hqk,hkd->hqd", probs, values, preferred_element_type=jnp.float32)
    mixed = mixed.astype(jnp.bfloat16).transpose(1, 0, 2).reshape(total_len, -1)
    return mixed, (queries, keys, values, log_total)


def attend_back(d_mixed, kept, key_valid):
    queries, keys, values, log_total = kept
    n_heads, total_len, head_dim = queries.shape
    scale = head_dim ** (-0.5)
    d_mixed = d_mixed.reshape(total_len, n_heads, head_dim).transpose(1, 0, 2)
    scores = jnp.einsum("hqd,hkd->hqk", queries, keys, preferred_element_type=jnp.float32) * scale
    scores = jnp.where(key_valid[None, None, :], scores, MASKED)
    probs = jnp.exp(scores - log_total)
    d_probs = jnp.einsum("hqd,hkd->hqk", d_mixed, values, preferred_element_type=jnp.float32)
    row_delta = jnp.sum(probs * d_probs, axis=-1, keepdims=True)
    d_scores = (probs * (d_probs - row_delta)).astype(jnp.bfloat16)
    probs = probs.astype(jnp.bfloat16)
    d_queries = jnp.einsum("hqk,hkd->hqd", d_scores, keys, preferred_element_type=jnp.float32) * scale
    d_keys = jnp.einsum("hqk,hqd->hkd", d_scores, queries, preferred_element_type=jnp.float32) * scale
    d_values = jnp.einsum("hqk,hqd->hkd", probs, d_mixed, preferred_element_type=jnp.float32)
    d_joined = jnp.stack([d_queries, d_keys, d_values]).astype(jnp.bfloat16)
    return d_joined.transpose(2, 1, 0, 3).reshape(total_len, -1)


def by_sequence(
    tokens,
    cotangent,
    seq_lengths,
    combined_weight,
    joined_bias,
    attention_out_weight,
    attention_out_bias,
    expand_weight,
    expand_bias,
    contract_weight,
    contract_bias,
    norm_gains,
    norm_shifts,
):
    n_layers, width, own_heads, _, head_dim = combined_weight.shape
    n_tp, n_ctx = lax.axis_size("tp"), lax.axis_size("ctx")
    n_rows = tokens.shape[1]
    total_len = n_rows * n_ctx
    own_seq = lax.axis_index("tp") * (tokens.shape[0] // n_tp) + lax.axis_index("ctx") // n_tp
    key_valid = jnp.arange(total_len) < seq_lengths[own_seq]

    flat_bias = jnp.concatenate(
        [
            joined_bias.transpose(0, 2, 1, 3).reshape(n_layers, 2, -1)[:, 0],
            joined_bias.transpose(0, 2, 1, 3).reshape(n_layers, 2, -1)[:, 1],
            expand_bias,
        ],
        axis=1,
    )
    flat_bias = lax.all_gather(flat_bias, "tp", axis=1)
    own_cols = own_heads * head_dim
    bias_q = flat_bias[..., :own_cols].reshape(n_layers, n_tp * own_heads, 1, head_dim)
    bias_v = flat_bias[..., own_cols : 2 * own_cols].reshape(bias_q.shape)
    bias_qkv = jnp.concatenate([bias_q, jnp.zeros_like(bias_q), bias_v], axis=2)
    bias_qkv = bias_qkv.reshape(n_layers, -1).astype(jnp.float32)
    bias_up = flat_bias[..., 2 * own_cols :].reshape(n_layers, -1).astype(jnp.float32)

    fetched = []
    last = None
    for layer_idx in range(n_layers):
        sources = (
            (fetch_columns, combined_weight[layer_idx].reshape(width, -1)),
            (fetch_rows, attention_out_weight[layer_idx]),
            (fetch_columns, expand_weight[layer_idx]),
            (fetch_rows, contract_weight[layer_idx]),
        )
        held = []
        for fetch, weight in sources:
            if last is not None:
                weight = after(weight, last)
            held.append(fetch(weight))
            last = held[-1]
        fetched.append(held)

    hidden = rows_of(tokens, "tp", 0).reshape(-1, width).astype(jnp.float32)
    saved = []
    for layer_idx in range(n_layers):
        w_qkv, w_out, w_up, w_down = fetched[layer_idx]
        hidden_low = hidden.astype(jnp.bfloat16)
        projected = (matmul(hidden_low, w_qkv) + bias_qkv[layer_idx]).astype(jnp.bfloat16)
        mixed, attn_kept = attend(to_heads(projected, n_tp), key_valid, head_dim)
        mixed = to_rows(mixed, n_tp)
        branch = matmul(mixed, w_out)
        normed, first_back = jax.vjp(
            normalize,
            hidden + branch + attention_out_bias[layer_idx],
            norm_gains[layer_idx, 0].astype(jnp.float32),
            norm_shifts[layer_idx, 0].astype(jnp.float32),
        )
        normed_low = normed.astype(jnp.bfloat16)
        before = matmul(normed_low, w_up) + bias_up[layer_idx]
        gated = smooth_gate(before).astype(jnp.bfloat16)
        hidden, second_back = jax.vjp(
            normalize,
            normed + matmul(gated, w_down) + contract_bias[layer_idx],
            norm_gains[layer_idx, 1].astype(jnp.float32),
            norm_shifts[layer_idx, 1].astype(jnp.float32),
        )
        saved.append((hidden_low, attn_kept, mixed, normed_low, before, gated, first_back, second_back))

    n_share = tokens.shape[0] // n_tp
    outputs = lax.all_gather(
        hidden.astype(jnp.bfloat16).reshape(n_share, n_rows, width), "tp", axis=0, tiled=True
    ).astype(jnp.float32)

    grad_now = rows_of(cotangent, "tp", 0).reshape(-1, width).astype(jnp.float32)
    reduced = [None] * n_layers
    small = [None] * n_layers
    for layer_idx in reversed(range(n_layers)):
        w_qkv, w_out, w_up, w_down = fetched[layer_idx]
        hidden_low, attn_kept, mixed, normed_low, before, gated, first_back, second_back = saved[layer_idx]
        d_resid_two, d_gain_two, d_shift_two = second_back(grad_now)
        d_two_low = d_resid_two.astype(jnp.bfloat16)
        d_down = matmul_tn(gated, d_two_low)
        d_gated = matmul_nt(d_two_low, w_down)
        d_before = jax.vjp(smooth_gate, before)[1](d_gated)[0].astype(jnp.bfloat16)
        d_up = matmul_tn(normed_low, d_before)
        d_normed = matmul_nt(d_before, w_up) + d_resid_two
        d_resid_one, d_gain_one, d_shift_one = first_back(d_normed)
        d_one_low = d_resid_one.astype(jnp.bfloat16)
        d_out = matmul_tn(mixed, d_one_low)
        d_mixed = matmul_nt(d_one_low, w_out).astype(jnp.bfloat16)
        d_joined = attend_back(to_heads(d_mixed, n_tp), attn_kept, key_valid)
        d_joined = to_rows(d_joined, n_tp)
        d_qkv = matmul_tn(hidden_low, d_joined)
        grad_now = matmul_nt(d_joined, w_qkv) + d_resid_one
        early = [reduce_rows(d_down), reduce_columns(d_up), reduce_rows(d_out)]
        late = reduce_columns(d_qkv)
        reduced[layer_idx] = (late, early[2], early[1], early[0])
        if layer_idx > 0:
            chained = lax.optimization_barrier((grad_now,))
            grad_now = chained[0]
        small[layer_idx] = (
            jnp.sum(d_joined.astype(jnp.float32), axis=0),
            jnp.sum(d_resid_one, axis=0),
            jnp.sum(d_before.astype(jnp.float32), axis=0),
            jnp.sum(d_resid_two, axis=0),
            d_gain_one,
            d_gain_two,
            d_shift_one,
            d_shift_two,
        )

    tokens_grad = lax.all_gather(
        grad_now.astype(jnp.bfloat16).reshape(n_share, n_rows, width), "tp", axis=0, tiled=True
    ).astype(jnp.float32)
    sizes = [entry.shape[0] for entry in small[0]]
    packed = jnp.stack([jnp.concatenate(entry) for entry in small])
    packed = lax.psum(packed, ("ctx", "tp"))
    pieces = []
    at = 0
    for size in sizes:
        pieces.append(packed[:, at : at + size])
        at += size
    d_bias = pieces[0].reshape(n_layers, n_tp * own_heads, 3, head_dim)[:, :, ::2, :]
    whole = [[spread(entry) for entry in layer] for layer in reduced]
    stacked = [jnp.stack([layer[member] for layer in whole]) for member in range(4)]
    return (
        outputs,
        tokens_grad,
        stacked[0].reshape(combined_weight.shape),
        rows_of(d_bias, "tp", 1),
        stacked[1],
        pieces[1],
        stacked[2],
        rows_of(pieces[2], "tp", 1),
        stacked[3],
        pieces[3],
        jnp.stack([pieces[4], pieces[5]], axis=1),
        jnp.stack([pieces[6], pieces[7]], axis=1),
    )


def solution(mesh):
    placed = (
        P(None, "ctx", None),
        P(None, "ctx", None),
        P(),
        P(None, None, "tp", None, None),
        P(None, "tp", None, None),
        P(None, "tp", None),
        P(),
        P(None, None, "tp"),
        P(None, "tp"),
        P(None, "tp", None),
        P(),
        P(),
        P(),
    )

    def chosen(tokens, *rest):
        n_seqs, n_ctx, n_tp = tokens.shape[0], mesh.shape["ctx"], mesh.shape["tp"]
        whole_heads = n_seqs == n_ctx and n_seqs % n_tp == 0
        return (by_sequence if whole_heads else on_device)(tokens, *rest)

    return jax.shard_map(
        chosen,
        mesh=mesh,
        in_specs=placed,
        out_specs=(
            P(None, "ctx", None),
            P(None, "ctx", None),
            P(None, None, "tp", None, None),
            P(None, "tp", None, None),
            P(None, "tp", None),
            P(),
            P(None, None, "tp"),
            P(None, "tp"),
            P(None, "tp", None),
            P(),
            P(),
            P(),
        ),
        check_vma=False,
    )
```

```python
import jax
import jax.numpy as jnp
from jax import lax
from jax.sharding import PartitionSpec as P

EPS = 1e-12
MASKED = -1e30


def normalize(resid, norm_gain, norm_shift):
    row_mean = jnp.mean(resid, axis=-1, keepdims=True)
    centred = resid - row_mean
    spread = jnp.mean(centred * centred, axis=-1, keepdims=True)
    return centred * lax.rsqrt(spread + EPS) * norm_gain + norm_shift


def smooth_gate(value):
    return (
        0.5
        * value
        * (1.0 + jnp.tanh(0.7978845608028654 * (value + 0.044715 * value * value * value)))
    )


def attention_scores(queries, key_rows, key_valid, scale):
    scores = (
        jnp.einsum("sqhd,skhd->shqk", queries, key_rows, preferred_element_type=jnp.float32) * scale
    )
    return jnp.where(key_valid[:, None, None, :], scores, MASKED)


def share_sum(partial_rows):
    return lax.psum_scatter(partial_rows, "tp", scatter_dimension=1, tiled=True)


def share_gather(rows_low):
    return lax.all_gather(rows_low, "tp", axis=1, tiled=True)


def take_share(full_rows):
    share_rows = full_rows.shape[1] // lax.axis_size("tp")
    return lax.dynamic_slice_in_dim(full_rows, lax.axis_index("tp") * share_rows, share_rows, 1)


def forward_layer(
    hidden,
    hidden_reduced,
    seq_lengths,
    combined_weight,
    joined_bias,
    attention_out_weight,
    attention_out_bias,
    expand_weight,
    expand_bias,
    contract_weight,
    contract_bias,
    norm_gains,
    norm_shifts,
):
    n_seqs, n_rows, width = hidden_reduced.shape
    n_heads = combined_weight.shape[1]
    head_dim = combined_weight.shape[3]
    scale = head_dim ** (-0.5)
    joined_flat = combined_weight.reshape(width, -1)
    combined_projected = jnp.einsum(
        "sbd,dc->sbc", hidden_reduced, joined_flat, preferred_element_type=jnp.float32
    )
    combined_projected = combined_projected.reshape(n_seqs, n_rows, n_heads, 3, head_dim)
    queries = (combined_projected[..., 0, :] + joined_bias[:, 0, :]).astype(jnp.bfloat16)
    key_rows = combined_projected[..., 1, :].astype(jnp.bfloat16)
    value_rows = (combined_projected[..., 2, :] + joined_bias[:, 1, :]).astype(jnp.bfloat16)
    all_keys, all_values = (
        lax.all_gather(key_rows.reshape(n_seqs, n_rows, -1), "ctx", axis=1, tiled=True),
        lax.all_gather(value_rows.reshape(n_seqs, n_rows, -1), "ctx", axis=1, tiled=True),
    )
    total_len = all_keys.shape[1]
    all_keys = all_keys.reshape(n_seqs, total_len, n_heads, head_dim)
    all_values = all_values.reshape(n_seqs, total_len, n_heads, head_dim)
    key_valid = jnp.arange(total_len)[None, :] < seq_lengths[:, None]
    scores = attention_scores(queries, all_keys, key_valid, scale)
    row_max = jnp.max(scores, axis=-1, keepdims=True)
    log_total = row_max + jnp.log(jnp.sum(jnp.exp(scores - row_max), axis=-1, keepdims=True))
    attn_probs = jnp.exp(scores - log_total).astype(jnp.bfloat16)
    merged_head_output = jnp.einsum(
        "shqk,skhd->sqhd", attn_probs, all_values, preferred_element_type=jnp.float32
    )
    merged_head_output = merged_head_output.astype(jnp.bfloat16).reshape(n_seqs, n_rows, -1)
    attention_branch = jnp.einsum(
        "sbc,cd->sbd", merged_head_output, attention_out_weight, preferred_element_type=jnp.float32
    )
    attention_branch = share_sum(attention_branch)
    normalized_rows, first_back = jax.vjp(
        normalize, hidden + attention_branch + attention_out_bias, norm_gains[0], norm_shifts[0]
    )
    normed_low = normalized_rows.astype(jnp.bfloat16)
    normed_low = share_gather(normed_low)
    before_activation = (
        jnp.einsum("sbd,df->sbf", normed_low, expand_weight, preferred_element_type=jnp.float32)
        + expand_bias
    )
    activated_hidden, gate_back = jax.vjp(smooth_gate, before_activation)
    gated_low = activated_hidden.astype(jnp.bfloat16)
    feedforward_branch = jnp.einsum(
        "sbf,fd->sbd", gated_low, contract_weight, preferred_element_type=jnp.float32
    )
    feedforward_branch = share_sum(feedforward_branch)
    result, second_back = jax.vjp(
        normalize,
        normalized_rows + feedforward_branch + contract_bias,
        norm_gains[1],
        norm_shifts[1],
    )
    kept = (
        hidden_reduced,
        queries,
        key_rows,
        value_rows,
        all_keys,
        all_values,
        key_valid,
        log_total,
        merged_head_output,
        normed_low,
        gated_low,
        first_back,
        gate_back,
        second_back,
    )
    return (result, kept)


def backward_layer(
    grad_out, kept, combined_weight, attention_out_weight, expand_weight, contract_weight
):
    (
        hidden_reduced,
        queries,
        key_rows,
        value_rows,
        all_keys,
        all_values,
        key_valid,
        log_total,
        merged_head_output,
        normed_low,
        gated_low,
        first_back,
        gate_back,
        second_back,
    ) = kept
    n_seqs, n_rows, n_heads, head_dim = queries.shape
    width = hidden_reduced.shape[2]
    total_len = all_keys.shape[1]
    scale = head_dim ** (-0.5)
    d_resid_two, d_gain_two, d_shift_two = second_back(grad_out)
    d_down_bias = jnp.sum(d_resid_two, axis=(0, 1))
    d_branch_two = d_resid_two.astype(jnp.bfloat16)
    d_branch_two = share_gather(d_branch_two)
    d_down = jnp.einsum("sbf,sbd->fd", gated_low, d_branch_two, preferred_element_type=jnp.float32)
    d_gated = jnp.einsum(
        "sbd,fd->sbf", d_branch_two, contract_weight, preferred_element_type=jnp.float32
    )
    d_pre_gate = gate_back(d_gated)[0].astype(jnp.bfloat16)
    d_up_bias = jnp.sum(d_pre_gate.astype(jnp.float32), axis=(0, 1))
    d_upward = jnp.einsum("sbd,sbf->df", normed_low, d_pre_gate, preferred_element_type=jnp.float32)
    d_normed = jnp.einsum(
        "sbf,df->sbd", d_pre_gate, expand_weight, preferred_element_type=jnp.float32
    )
    d_normed = share_sum(d_normed) + d_resid_two
    d_resid_one, d_gain_one, d_shift_one = first_back(d_normed)
    d_mixer_bias = jnp.sum(d_resid_one, axis=(0, 1))
    d_branch = d_resid_one.astype(jnp.bfloat16)
    d_branch = share_gather(d_branch)
    d_mixer = jnp.einsum(
        "sbc,sbd->cd", merged_head_output, d_branch, preferred_element_type=jnp.float32
    )
    d_mixed = jnp.einsum(
        "sbd,cd->sbc", d_branch, attention_out_weight, preferred_element_type=jnp.float32
    )
    d_mixed = d_mixed.astype(jnp.bfloat16).reshape(n_seqs, n_rows, n_heads, head_dim)
    scores = attention_scores(queries, all_keys, key_valid, scale)
    probs_full = jnp.exp(scores - log_total)
    d_probs = jnp.einsum("sqhd,skhd->shqk", d_mixed, all_values, preferred_element_type=jnp.float32)
    row_delta = jnp.sum(probs_full * d_probs, axis=-1, keepdims=True)
    d_scores = (probs_full * (d_probs - row_delta)).astype(jnp.bfloat16)
    d_queries = (
        jnp.einsum("shqk,skhd->sqhd", d_scores, all_keys, preferred_element_type=jnp.float32)
        * scale
    )
    d_queries = d_queries.astype(jnp.bfloat16)
    key_part = (
        jnp.einsum("shqk,sqhd->skhd", d_scores, queries, preferred_element_type=jnp.float32) * scale
    )
    value_part = jnp.einsum(
        "shqk,sqhd->skhd",
        probs_full.astype(jnp.bfloat16),
        d_mixed,
        preferred_element_type=jnp.float32,
    )
    d_keys, d_values = (
        lax.psum_scatter(
            key_part.reshape(n_seqs, total_len, -1), "ctx", scatter_dimension=1, tiled=True
        ),
        lax.psum_scatter(
            value_part.reshape(n_seqs, total_len, -1), "ctx", scatter_dimension=1, tiled=True
        ),
    )
    d_keys = d_keys.reshape(n_seqs, n_rows, n_heads, head_dim)
    d_values = d_values.reshape(n_seqs, n_rows, n_heads, head_dim)
    d_keys = d_keys.astype(jnp.bfloat16)
    d_values = d_values.astype(jnp.bfloat16)
    d_joined_bias = jnp.stack(
        [
            jnp.sum(d_queries.astype(jnp.float32), axis=(0, 1)),
            jnp.sum(d_values.astype(jnp.float32), axis=(0, 1)),
        ],
        axis=1,
    )
    d_joined_out = jnp.stack([d_queries, d_keys, d_values], axis=3).reshape(n_seqs, n_rows, -1)
    d_joined = jnp.einsum(
        "sbd,sbc->dc", hidden_reduced, d_joined_out, preferred_element_type=jnp.float32
    )
    d_joined = d_joined.reshape(width, n_heads, 3, head_dim)
    d_hidden = jnp.einsum(
        "sbc,dc->sbd",
        d_joined_out,
        combined_weight.reshape(width, -1),
        preferred_element_type=jnp.float32,
    )
    d_hidden = share_sum(d_hidden) + d_resid_one
    small_grads = (
        d_mixer_bias,
        d_down_bias,
        jnp.stack([d_gain_one, d_gain_two]),
        jnp.stack([d_shift_one, d_shift_two]),
    )
    small_grads = lax.psum(
        (
            small_grads[0],
            small_grads[1],
            small_grads[2].astype(jnp.float32),
            small_grads[3].astype(jnp.float32),
        ),
        "tp",
    )
    grads = (
        d_joined,
        d_joined_bias,
        d_mixer,
        small_grads[0],
        d_upward,
        d_up_bias,
        d_down,
        small_grads[1],
        small_grads[2],
        small_grads[3],
    )
    return (d_hidden, grads)


def sum_layer(grads):
    return lax.psum(
        (
            grads[0],
            grads[1],
            grads[2],
            grads[3],
            grads[4],
            grads[5],
            grads[6],
            grads[7],
            grads[8],
            grads[9],
        ),
        "ctx",
    )


def on_device(
    tokens,
    cotangent,
    seq_lengths,
    combined_weight,
    joined_bias,
    attention_out_weight,
    attention_out_bias,
    expand_weight,
    expand_bias,
    contract_weight,
    contract_bias,
    norm_gains,
    norm_shifts,
):
    params = (
        combined_weight,
        joined_bias,
        attention_out_weight,
        attention_out_bias,
        expand_weight,
        expand_bias,
        contract_weight,
        contract_bias,
        norm_gains,
        norm_shifts,
    )
    n_layers = combined_weight.shape[0]
    hidden = tokens.astype(jnp.float32)
    hidden_reduced = tokens
    hidden = take_share(hidden)
    saved = []
    for layer_idx in range(n_layers):
        hidden, kept = forward_layer(
            hidden, hidden_reduced, seq_lengths, *[weight[layer_idx] for weight in params]
        )
        saved.append(kept)
        if layer_idx + 1 < n_layers:
            hidden_reduced = hidden.astype(jnp.bfloat16)
            hidden_reduced = share_gather(hidden_reduced)
    grad_now = cotangent.astype(jnp.float32)
    grad_now = take_share(grad_now)
    collected = []
    for layer_idx in reversed(range(n_layers)):
        grad_now, grads = backward_layer(
            grad_now,
            saved[layer_idx],
            combined_weight[layer_idx],
            attention_out_weight[layer_idx],
            expand_weight[layer_idx],
            contract_weight[layer_idx],
        )
        grads = sum_layer(grads)
        collected.insert(0, grads)
    stacked = tuple((jnp.stack([entry[member] for entry in collected]) for member in range(10)))
    hidden, grad_now = (
        lax.all_gather(hidden, "tp", axis=1, tiled=True),
        lax.all_gather(grad_now, "tp", axis=1, tiled=True),
    )
    return (
        hidden,
        grad_now,
        stacked[0],
        stacked[1],
        stacked[2],
        stacked[3],
        stacked[4],
        stacked[5],
        stacked[6],
        stacked[7],
        stacked[8],
        stacked[9],
    )

def rows_of(array, axis_name, dim):
    share = array.shape[dim] // lax.axis_size(axis_name)
    return lax.dynamic_slice_in_dim(array, lax.axis_index(axis_name) * share, share, dim)


def after(value, *earlier):
    return lax.optimization_barrier((value,) + earlier)[0]


def padded(array, width):
    return jnp.pad(array, [(0, 0)] * (array.ndim - 1) + [(0, width - array.shape[-1])])


def side_by_side(part):
    return part.transpose(1, 0, 2).reshape(part.shape[1], -1)


def fetch_columns(part):
    return lax.all_gather(side_by_side(part), "ctx", axis=0, tiled=True)


def fetch_rows(part):
    whole = lax.all_gather(part, "ctx", axis=1, tiled=True)
    return whole.reshape(-1, whole.shape[2])


def blocks_of_columns(grad, n_ctx, n_tp):
    blocks = grad.astype(jnp.bfloat16).reshape(n_ctx, grad.shape[0] // n_ctx, n_tp, -1)
    return blocks.transpose(0, 2, 1, 3)


def blocks_of_rows(grad, n_ctx, n_tp):
    blocks = grad.astype(jnp.bfloat16).reshape(n_tp, n_ctx, -1, grad.shape[1])
    return blocks.transpose(1, 0, 2, 3)


def sum_blocks(blocks, axis_name):
    blocks = blocks.reshape(blocks.shape[0], -1, blocks.shape[-1])
    moved = lax.all_to_all(blocks, axis_name, 0, 0, tiled=True)
    return jnp.sum(moved.astype(jnp.float32), axis=0)


def sum_everywhere(small):
    for axis_name in ("tp", "ctx"):
        small = jnp.sum(lax.all_gather(small, axis_name, axis=0), axis=0)
    return small


def to_heads(rows, n_groups):
    n_rows = rows.shape[0] * n_groups // lax.axis_size("ctx")
    blocks = rows.reshape(-1, n_rows, n_groups, rows.shape[1] // n_groups)
    blocks = blocks.transpose(0, 2, 1, 3).reshape(-1, n_rows, blocks.shape[3])
    blocks = lax.all_to_all(blocks, "ctx", 0, 0, tiled=True)
    return blocks.reshape(-1, blocks.shape[2])


def to_rows(whole, n_groups):
    n_ctx = lax.axis_size("ctx")
    blocks = whole.reshape(n_ctx, whole.shape[0] // n_ctx, whole.shape[1])
    blocks = lax.all_to_all(blocks, "ctx", 0, 0, tiled=True)
    blocks = blocks.reshape(n_ctx // n_groups, n_groups, blocks.shape[1], blocks.shape[2])
    blocks = blocks.transpose(0, 2, 1, 3)
    return blocks.reshape(-1, n_groups * whole.shape[1])


def matmul(left, right):
    return jnp.dot(left, right, preferred_element_type=jnp.float32)


def matmul_tn(left, right):
    return lax.dot_general(left, right, (((0,), (0,)), ((), ())), preferred_element_type=jnp.float32)


def matmul_nt(left, right):
    return lax.dot_general(left, right, (((1,), (1,)), ((), ())), preferred_element_type=jnp.float32)


def attend(joined, key_valid, head_dim):
    total_len = joined.shape[0]
    scale = head_dim ** (-0.5)
    parts = joined.reshape(total_len, -1, 3, head_dim).transpose(2, 1, 0, 3)
    queries, keys, values = parts[0], parts[1], parts[2]
    scores = jnp.einsum("hqd,hkd->hqk", queries, keys, preferred_element_type=jnp.float32) * scale
    scores = jnp.where(key_valid[None, None, :], scores, MASKED)
    row_max = jnp.max(scores, axis=-1, keepdims=True)
    log_total = row_max + jnp.log(jnp.sum(jnp.exp(scores - row_max), axis=-1, keepdims=True))
    probs = jnp.exp(scores - log_total).astype(jnp.bfloat16)
    mixed = jnp.einsum("hqk,hkd->hqd", probs, values, preferred_element_type=jnp.float32)
    mixed = mixed.astype(jnp.bfloat16).transpose(1, 0, 2).reshape(total_len, -1)
    return mixed, (queries, keys, values, log_total)


def attend_back(d_mixed, kept, key_valid):
    queries, keys, values, log_total = kept
    n_heads, total_len, head_dim = queries.shape
    scale = head_dim ** (-0.5)
    d_mixed = d_mixed.reshape(total_len, n_heads, head_dim).transpose(1, 0, 2)
    scores = jnp.einsum("hqd,hkd->hqk", queries, keys, preferred_element_type=jnp.float32) * scale
    scores = jnp.where(key_valid[None, None, :], scores, MASKED)
    probs = jnp.exp(scores - log_total)
    d_probs = jnp.einsum("hqd,hkd->hqk", d_mixed, values, preferred_element_type=jnp.float32)
    row_delta = jnp.sum(probs * d_probs, axis=-1, keepdims=True)
    d_scores = (probs * (d_probs - row_delta)).astype(jnp.bfloat16)
    probs = probs.astype(jnp.bfloat16)
    d_queries = jnp.einsum("hqk,hkd->hqd", d_scores, keys, preferred_element_type=jnp.float32) * scale
    d_keys = jnp.einsum("hqk,hqd->hkd", d_scores, queries, preferred_element_type=jnp.float32) * scale
    d_values = jnp.einsum("hqk,hqd->hkd", probs, d_mixed, preferred_element_type=jnp.float32)
    d_joined = jnp.stack([d_queries, d_keys, d_values]).astype(jnp.bfloat16)
    return d_joined.transpose(2, 1, 0, 3).reshape(total_len, -1)


def by_sequence(
    tokens,
    cotangent,
    seq_lengths,
    combined_weight,
    joined_bias,
    attention_out_weight,
    attention_out_bias,
    expand_weight,
    expand_bias,
    contract_weight,
    contract_bias,
    norm_gains,
    norm_shifts,
):
    n_layers, width, own_heads, _, head_dim = combined_weight.shape
    n_tp, n_ctx = lax.axis_size("tp"), lax.axis_size("ctx")
    n_rows = tokens.shape[1]
    total_len = n_rows * n_ctx
    own_seq = lax.axis_index("tp") * (tokens.shape[0] // n_tp) + lax.axis_index("ctx") // n_tp
    key_valid = jnp.arange(total_len) < seq_lengths[own_seq]

    flat_bias = jnp.concatenate(
        [
            joined_bias.transpose(0, 2, 1, 3).reshape(n_layers, 2, -1)[:, 0],
            joined_bias.transpose(0, 2, 1, 3).reshape(n_layers, 2, -1)[:, 1],
            expand_bias,
        ],
        axis=1,
    )
    flat_bias = lax.all_gather(flat_bias, "tp", axis=1)
    own_cols = own_heads * head_dim
    bias_q = flat_bias[..., :own_cols].reshape(n_layers, n_tp * own_heads, 1, head_dim)
    bias_v = flat_bias[..., own_cols : 2 * own_cols].reshape(bias_q.shape)
    bias_qkv = jnp.concatenate([bias_q, jnp.zeros_like(bias_q), bias_v], axis=2)
    bias_qkv = bias_qkv.reshape(n_layers, -1).astype(jnp.float32)
    bias_up = flat_bias[..., 2 * own_cols :].reshape(n_layers, -1).astype(jnp.float32)

    ends = [0]

    def fetch_parts(layer_idx, *earlier):
        sources = (
            padded(rows_of(combined_weight[layer_idx].reshape(width, -1), "ctx", 0), width),
            rows_of(attention_out_weight[layer_idx], "ctx", 0),
            rows_of(expand_weight[layer_idx], "ctx", 0),
            rows_of(contract_weight[layer_idx], "ctx", 0),
        )
        del ends[1:]
        for source in sources:
            ends.append(ends[-1] + source.shape[0])
        part = lax.all_gather(after(jnp.concatenate(sources, axis=0), *earlier), "tp", axis=0)
        own = [part[:, ends[i] : ends[i + 1]] for i in range(4)]
        own[0] = own[0][:, :, : 3 * own_cols]
        return own

    fetched = []
    own = fetch_parts(0)
    w_qkv = fetch_columns(own[0])

    hidden = rows_of(tokens, "tp", 0).reshape(-1, width).astype(jnp.float32)
    saved = []
    for layer_idx in range(n_layers):
        hidden_low = hidden.astype(jnp.bfloat16)
        projected = (matmul(hidden_low, w_qkv) + bias_qkv[layer_idx]).astype(jnp.bfloat16)
        later = [after(part, projected) for part in own[1:]]
        w_out, w_up = fetch_rows(later[0]), fetch_columns(later[1])
        w_down = fetch_rows(later[2])
        fetched.append((w_qkv, w_out, w_up, w_down))
        if layer_idx + 1 < n_layers:
            own = fetch_parts(layer_idx + 1, projected)
        mixed, attn_kept = attend(to_heads(projected, n_tp), key_valid, head_dim)
        mixed = to_rows(mixed, n_tp)
        if layer_idx + 1 < n_layers:
            own = [after(part, mixed) for part in own]
            w_qkv = fetch_columns(own[0])
        branch = matmul(mixed, w_out)
        normed, first_back = jax.vjp(
            normalize,
            hidden + branch + attention_out_bias[layer_idx],
            norm_gains[layer_idx, 0].astype(jnp.float32),
            norm_shifts[layer_idx, 0].astype(jnp.float32),
        )
        normed_low = normed.astype(jnp.bfloat16)
        before = matmul(normed_low, w_up) + bias_up[layer_idx]
        gated = smooth_gate(before).astype(jnp.bfloat16)
        hidden, second_back = jax.vjp(
            normalize,
            normed + matmul(gated, w_down) + contract_bias[layer_idx],
            norm_gains[layer_idx, 1].astype(jnp.float32),
            norm_shifts[layer_idx, 1].astype(jnp.float32),
        )
        saved.append((hidden_low, attn_kept, mixed, normed_low, before, gated, first_back, second_back))

    n_share = tokens.shape[0] // n_tp
    outputs = lax.all_gather(
        hidden.astype(jnp.bfloat16).reshape(n_share, n_rows, width), "tp", axis=0, tiled=True
    ).astype(jnp.float32)

    grad_now = rows_of(cotangent, "tp", 0).reshape(-1, width).astype(jnp.float32)
    reduced = [None] * n_layers
    small = [None] * n_layers
    summed_before = None
    for layer_idx in reversed(range(n_layers)):
        w_qkv, w_out, w_up, w_down = fetched[layer_idx]
        hidden_low, attn_kept, mixed, normed_low, before, gated, first_back, second_back = saved[layer_idx]
        d_resid_two, d_gain_two, d_shift_two = second_back(grad_now)
        d_two_low = d_resid_two.astype(jnp.bfloat16)
        d_down = matmul_tn(gated, d_two_low)
        d_gated = matmul_nt(d_two_low, w_down)
        d_before = jax.vjp(smooth_gate, before)[1](d_gated)[0].astype(jnp.bfloat16)
        d_up = matmul_tn(normed_low, d_before)
        d_normed = matmul_nt(d_before, w_up) + d_resid_two
        d_resid_one, d_gain_one, d_shift_one = first_back(d_normed)
        d_one_low = d_resid_one.astype(jnp.bfloat16)
        d_out = matmul_tn(mixed, d_one_low)
        d_mixed = matmul_nt(d_one_low, w_out).astype(jnp.bfloat16)
        d_joined = attend_back(to_heads(d_mixed, n_tp), attn_kept, key_valid)
        if summed_before is not None:
            d_joined, summed_before = lax.optimization_barrier((d_joined, summed_before))
        d_joined = to_rows(d_joined, n_tp)
        d_qkv = matmul_tn(hidden_low, d_joined)
        grad_now = matmul_nt(d_joined, w_qkv) + d_resid_one
        blocks = [
            padded(blocks_of_columns(d_qkv, n_ctx, n_tp), width),
            blocks_of_rows(d_out, n_ctx, n_tp),
            blocks_of_columns(d_up, n_ctx, n_tp),
            blocks_of_rows(d_down, n_ctx, n_tp),
        ]
        summed = sum_blocks(jnp.concatenate(blocks, axis=2), "ctx")
        summed = summed.astype(jnp.bfloat16)
        summed_before = summed
        summed = sum_blocks(summed.reshape(n_tp, -1, width), "tp").astype(jnp.bfloat16)
        reduced[layer_idx] = lax.all_gather(summed, "ctx", axis=0)
        small[layer_idx] = (
            jnp.sum(d_joined.astype(jnp.float32), axis=0),
            jnp.sum(d_resid_one, axis=0),
            jnp.sum(d_before.astype(jnp.float32), axis=0),
            jnp.sum(d_resid_two, axis=0),
            d_gain_one,
            d_gain_two,
            d_shift_one,
            d_shift_two,
        )

    tokens_grad = lax.all_gather(
        grad_now.astype(jnp.bfloat16).reshape(n_share, n_rows, width), "tp", axis=0, tiled=True
    ).astype(jnp.float32)
    sizes = [entry.shape[0] for entry in small[0]]
    packed = jnp.stack([jnp.concatenate(entry) for entry in small])
    packed = sum_everywhere(packed)
    pieces = []
    at = 0
    for size in sizes:
        pieces.append(packed[:, at : at + size])
        at += size
    d_bias = pieces[0].reshape(n_layers, n_tp * own_heads, 3, head_dim)[:, :, ::2, :]
    whole = []
    for layer in reduced:
        pieces_of = [layer[:, ends[i] : ends[i + 1]].astype(jnp.float32) for i in range(4)]
        pieces_of[0] = pieces_of[0][:, :, : 3 * own_cols]
        whole.append([piece.reshape(-1, piece.shape[2]) for piece in pieces_of])
    stacked = [jnp.stack([layer[member] for layer in whole]) for member in range(4)]
    return (
        outputs,
        tokens_grad,
        stacked[0].reshape(combined_weight.shape),
        rows_of(d_bias, "tp", 1),
        stacked[1],
        pieces[1],
        stacked[2],
        rows_of(pieces[2], "tp", 1),
        stacked[3],
        pieces[3],
        jnp.stack([pieces[4], pieces[5]], axis=1),
        jnp.stack([pieces[6], pieces[7]], axis=1),
    )


def solution(mesh):
    placed = (
        P(None, "ctx", None),
        P(None, "ctx", None),
        P(),
        P(None, None, "tp", None, None),
        P(None, "tp", None, None),
        P(None, "tp", None),
        P(),
        P(None, None, "tp"),
        P(None, "tp"),
        P(None, "tp", None),
        P(),
        P(),
        P(),
    )

    def chosen(tokens, *rest):
        n_seqs, n_ctx, n_tp = tokens.shape[0], mesh.shape["ctx"], mesh.shape["tp"]
        whole_heads = n_seqs == n_ctx and n_seqs % n_tp == 0
        return (by_sequence if whole_heads else on_device)(tokens, *rest)

    return jax.shard_map(
        chosen,
        mesh=mesh,
        in_specs=placed,
        out_specs=(
            P(None, "ctx", None),
            P(None, "ctx", None),
            P(None, None, "tp", None, None),
            P(None, "tp", None, None),
            P(None, "tp", None),
            P(),
            P(None, None, "tp"),
            P(None, "tp"),
            P(None, "tp", None),
            P(),
            P(),
            P(),
        ),
        check_vma=False,
    )
```
